32 devices in a mesh: bunch: 16 (over z, x, core), dom: 2 (over y).
Axes of the slice: x: 2, y: 2, z: 4, core: 2. Of those that a mesh axis runs over, the one named last changes fastest.
Arguments:
- coords: float32 [4, 128, 65536], P(None, 'bunch', 'dom'), may hold values from -6 to 6
- slice_index: int32 [128, 65536], P('bunch', 'dom'), may hold values from 0 to 511
- fill: int32 [1792], P('bunch'), may hold values 0 or 1
- untracked_slot_centres: float32 [2, 1792], P(None, 'bunch'), may hold values from -0.046875 to 0.046875
- wake: float32 [4, 512, 64], replicated, may hold values from -0.75 to 0.75
- term_decay_factor: float32 [2, 8], replicated, may hold values from 0 to 1, as said below
- lr_coef: float32 [2, 8], replicated, may hold values from 0.5 to 5
- tunes: float32 [2], replicated, may hold values from 0.26 to 0.32
- chroma: float32 [2], replicated, may hold values from -3 to 3
Outputs:
- coords_out: float32 [4, 128, 65536], P(None, 'bunch', 'dom')
The draws below stay inside these ranges and needn't reach their ends.
Inputs may be any that keep to these rules, and one draw needn't show every extreme that they name: `term_decay_factor`: rates of at least 0.1 / 1792.
All inputs are finite; a program needn't handle non-finite values. No bound on the sum of `fill` on one device may be relied on, other than what follows from the above.
Results may differ from the reference program's by a relative error of at most 0.0002.
Values sent between devices are 32-bit elements; how exact they have to be, the bound alone decides.
A program may use at most 128 MiB of HBM per device.

```python
import math
import jax
import jax.numpy as jnp
from jax import lax

SLICES = 512
BAND = 64
WAKE_TERMS = 8
SLOT_DEV = 112
BUNCH_DEV = 8
SLOT_COUNT = 1792
NBUNCH = 128
NPART = 65536
N_BUNCH = 16


def draw_term_decay_factor(key, part):
    slow_random_key = jax.random.fold_in(key, 11)
    key_fast = jax.random.fold_in(key, 12)
    key_pick = jax.random.fold_in(key, 13)
    fast_rate = jax.random.uniform(key_fast, (2, WAKE_TERMS), jnp.float32, 1.0 / 50.0, 1.0 / 30.0)
    slow_logarithm = jax.random.uniform(slow_random_key, (2, WAKE_TERMS), jnp.float32, math.log(0.1 / SLOT_COUNT), math.log(2.0 / SLOT_COUNT))
    slow_decay_rate = jnp.exp(slow_logarithm)
    chosen = jax.random.bernoulli(key_pick, 0.5, (2, WAKE_TERMS))
    return jnp.where(chosen, fast_rate, slow_decay_rate).astype(jnp.float32)


def plant(drawn, rng, least, high):
    longest = drawn.shape.index(max(drawn.shape))
    spots = []
    for shift in (0, 1):
        where = [jax.random.randint(jax.random.fold_in(rng, axis), (), 0, length) for axis, length in enumerate(drawn.shape)]
        where[longest] = (where[longest] + shift) % drawn.shape[longest]
        spots.append(tuple(where))
    return drawn.at[spots[0]].set(least).at[spots[1]].set(high)


def level_of(stream_key, dims, pieces, least, largest):
    loudness, own = 1.0, jax.random.fold_in(stream_key, 6)
    for position, blocks in pieces:
        steps = jnp.exp(jax.random.uniform(jax.random.fold_in(own, position), (blocks,), jnp.float32, least / len(pieces), largest / len(pieces)))
        loudness = loudness * jnp.repeat(steps, dims[position] // blocks).reshape([-1 if axis == position else 1 for axis in range(len(dims))])
    return loudness


def centred(key, shape, scale, limit, cuts=(), kind=jnp.bfloat16):
    array = scale * jax.random.normal(key, shape, jnp.float32)
    if cuts:
        array = array * level_of(key, shape, cuts, -0.22, 0.18)
    return jnp.clip(array, -limit, limit).astype(kind)


def setup_inputs(seed: int = 0) -> dict:
    key_of = jax.random.split(jax.random.key(seed), 10)
    coords = centred(key_of[0], (4, NBUNCH, NPART), 1.0, 6.0, ((1, 16), (2, 2)), jnp.float32)
    slice_index = plant(jax.random.randint(key_of[1], (NBUNCH, NPART), 0, SLICES), jax.random.fold_in(key_of[1], 1), 0, SLICES - 1).astype(jnp.int32)
    fill = plant((jax.random.randint(key_of[2], (SLOT_COUNT,), 0, 5) < 4).astype(jnp.int32), jax.random.fold_in(key_of[2], 1), 0, 1)
    untracked_slot_centres = centred(key_of[3], (2, SLOT_COUNT), 0.003, 0.046875, ((1, 16),), jnp.float32)
    wake = centred(key_of[4], (4, SLICES, BAND), BAND ** -0.5, 0.75, (), jnp.float32)
    term_decay_factor = draw_term_decay_factor(jax.random.fold_in(key_of[9], 71), 0)
    lr_coef = jnp.clip(jnp.exp(jax.random.uniform(key_of[6], (2, WAKE_TERMS), jnp.float32, math.log(0.5), math.log(5.0))), 0.5, 5.0)
    tunes = jnp.clip(jax.random.uniform(key_of[7], (2,), jnp.float32, 0.26, 0.32), 0.26, 0.32)
    chroma = jnp.clip(jax.random.uniform(key_of[8], (2,), jnp.float32, -3.0, 3.0), -3.0, 3.0)
    return dict(coords=coords, slice_index=slice_index, fill=fill, untracked_slot_centres=untracked_slot_centres, wake=wake, term_decay_factor=term_decay_factor, lr_coef=lr_coef, tunes=tunes, chroma=chroma)


def reference(coords, slice_index, fill, untracked_slot_centres, wake, term_decay_factor, lr_coef, tunes, chroma):
    pos_x, mom_x, pos_y, mom_y = coords[0], coords[1], coords[2], coords[3]
    segment = (jnp.arange(NBUNCH, dtype=jnp.int32)[:, None] * SLICES + slice_index).reshape(-1)
    scale_moment = SLICES / NPART

    def deposit(values):
        summed = jax.ops.segment_sum(values.reshape(-1), segment, num_segments=NBUNCH * SLICES)
        return summed.reshape(NBUNCH, SLICES) * scale_moment

    moments = jnp.stack([deposit(jnp.ones_like(pos_x)), deposit(pos_x), deposit(pos_y)], axis=1)
    source = jnp.stack([moments[:, 1], moments[:, 0], moments[:, 2], moments[:, 0]], axis=1)
    padded = jnp.pad(source, ((0, 0), (0, 0), (BAND, 0)))

    def add_lag(lag, total):
        start = (BAND - lag).astype(jnp.int32)
        shifted = lax.dynamic_slice_in_dim(padded, start, SLICES, 2)
        column = lax.dynamic_slice_in_dim(wake, lag.astype(jnp.int32), 1, 2)[:, :, 0]
        return total + column[None] * shifted

    slice_kick = lax.fori_loop(0, BAND, add_lag, jnp.zeros((NBUNCH, 4, SLICES), jnp.float32))
    tracked = jnp.sum(moments[:, 1:3], axis=2) / SLICES
    others = jnp.transpose(untracked_slot_centres).reshape(N_BUNCH, SLOT_DEV, 2)
    combined_result = jnp.concatenate([tracked.reshape(N_BUNCH, BUNCH_DEV, 2), others[:, BUNCH_DEV:]], axis=1)
    bunch_centre = fill.astype(jnp.float32)[:, None] * combined_result.reshape(SLOT_COUNT, 2)

    particle_position = jnp.arange(SLOT_COUNT, dtype=jnp.float32)
    leading_weight = jnp.exp(-term_decay_factor[None] * (SLOT_COUNT - 1 - particle_position)[:, None, None])
    initial_state = jnp.sum(leading_weight * bunch_centre[:, :, None], axis=0) / (1.0 - jnp.exp(-term_decay_factor * SLOT_COUNT))
    factor = jnp.exp(-term_decay_factor)

    def advance(carry, value):
        return factor * carry + value[:, None], carry

    final_carry, linear = lax.scan(advance, jnp.zeros_like(term_decay_factor), bunch_centre)
    state = jnp.exp(-term_decay_factor[None] * particle_position[:, None, None]) * initial_state[None] + linear
    state = state.reshape(N_BUNCH, SLOT_DEV, 2, WAKE_TERMS)[:, :BUNCH_DEV].reshape(NBUNCH, 2, WAKE_TERMS)
    long_kick = jnp.sum(state * lr_coef[None], axis=2)

    kick_dx = jnp.take_along_axis(slice_kick[:, 0], slice_index, axis=1)
    kick_qx = jnp.take_along_axis(slice_kick[:, 1], slice_index, axis=1)
    kick_dy = jnp.take_along_axis(slice_kick[:, 2], slice_index, axis=1)
    kick_qy = jnp.take_along_axis(slice_kick[:, 3], slice_index, axis=1)
    mom_xk = mom_x + kick_dx + kick_qx * pos_x + long_kick[:, 0:1]
    mom_yk = mom_y + kick_dy + kick_qy * pos_y + long_kick[:, 1:2]
    slice_pos = 2.0 * (slice_index.astype(jnp.float32) + 0.5) / SLICES - 1.0
    phase_x = 2.0 * math.pi * tunes[0] + chroma[0] * slice_pos
    phase_y = 2.0 * math.pi * tunes[1] + chroma[1] * slice_pos
    cos_x, sin_x = jnp.cos(phase_x), jnp.sin(phase_x)
    cos_y, sin_y = jnp.cos(phase_y), jnp.sin(phase_y)
    return jnp.stack([cos_x * pos_x + sin_x * mom_xk, cos_x * mom_xk - sin_x * pos_x,
                      cos_y * pos_y + sin_y * mom_yk, cos_y * mom_yk - sin_y * pos_y], axis=0)
```

```python
import functools
import math

import jax
import jax.numpy as jnp
from jax import lax
from jax.experimental import pallas as pl
from jax.experimental.pallas import tpu as pltpu
from jax.sharding import PartitionSpec as P

SLICES = 512
BAND = 64
LANES = 128
PIECES = SLICES // LANES
LOW = 64
HIGH = SLICES // LOW
MESH = pl.DeviceIdType.MESH


def rows_sum(value):
    return jnp.sum(value, axis=0, keepdims=True)


def lanes_sum(value):
    return jnp.sum(value, axis=1, keepdims=True)


def deposit_kernel(
    n_cycle,
    n_dom,
    chunk,
    step_len,
    coords,
    index,
    fill,
    others,
    wake,
    decay,
    coef,
    tunes,
    chroma,
    tables,
    phases,
    x_buf,
    y_buf,
    i_buf,
    wake_t,
    grid_sum,
    slots,
    outgoing,
    block_own,
    block_got,
    mine,
    theirs,
    padded,
    in_sem,
    block_send,
    block_recv,
    dom_send,
    dom_recv,
):
    bunch_dev, part_dev = x_buf.shape
    slot_dev = fill.shape[1]
    chunks = part_dev // chunk
    me_b, me_d = lax.axis_index("bunch"), lax.axis_index("dom")

    def loads(step):
        where = pl.ds(pl.multiple_of(step * chunk, chunk), chunk)
        return (
            pltpu.make_async_copy(coords.at[0, :, where], x_buf.at[:, where], in_sem.at[0, step]),
            pltpu.make_async_copy(coords.at[2, :, where], y_buf.at[:, where], in_sem.at[1, step]),
            pltpu.make_async_copy(index.at[:, where], i_buf.at[:, where], in_sem.at[2, step]),
        )

    for plane in range(3):
        for step in range(chunks):
            loads(step)[plane].start()

    cycle_peers = [(lax.rem(me_b + k, n_cycle), me_d) for k in range(1, n_cycle)]
    dom_peers = [(me_b, lax.rem(me_d + k, n_dom)) for k in range(1, n_dom)]
    barrier = pltpu.get_barrier_semaphore()
    for peer in cycle_peers + dom_peers:
        pl.semaphore_signal(barrier, inc=1, device_id=peer, device_id_type=MESH)

    lane = lax.broadcasted_iota(jnp.int32, (8, LANES), 1)
    row = lax.broadcasted_iota(jnp.int32, (8, LANES), 0)
    second = lane >= 64
    half = jnp.where(second, lane - 64, lane)
    half_f = half.astype(jnp.float32)
    zeros = jnp.zeros((8, LANES), jnp.float32)

    def by_row(ref, plane):
        built = zeros
        for term in range(8):
            built = jnp.where(row == term, ref[plane, term], built)
        return built

    decay_x, decay_y = by_row(decay, 0), by_row(decay, 1)
    decay_both = jnp.where(second, decay_y, decay_x)
    coef_both = jnp.where(second, by_row(coef, 1), by_row(coef, 0))
    back = (slot_dev - 1 - lane).astype(jnp.float32)
    inside = lane < slot_dev
    back = jnp.where(inside, back, 0.0)
    tail_x = jnp.where(inside, jnp.exp(-decay_x * back), 0.0)
    tail_y = jnp.where(inside, jnp.exp(-decay_y * back), 0.0)
    block_decay = jnp.exp(-decay_both * slot_dev)
    closing = 1.0 - jnp.exp(-decay_both * (slot_dev * n_cycle))
    ahead = coef_both * jnp.exp(-decay_both * half_f)

    lower = row < 4
    chroma_rows = jnp.where(lower, chroma[0], chroma[1])
    tune_rows = jnp.where(lower, tunes[0], tunes[1])
    fine = chroma_rows * (lane.astype(jnp.float32) * (2.0 / SLICES))
    first = 2.0 * ((lane & 3).astype(jnp.float32) * LANES + 0.5) / SLICES - 1.0
    coarse = 2.0 * math.pi * tune_rows + chroma_rows * first
    fine_cos, fine_sin = jnp.cos(fine), jnp.sin(fine)
    coarse_cos, coarse_sin = jnp.cos(coarse), jnp.sin(coarse)
    for plane in range(2):
        at = 4 * plane
        base = plane * (2 + 2 * PIECES)
        phases[base] = jnp.broadcast_to(fine_cos[at : at + 1], (8, LANES))
        phases[base + 1] = jnp.broadcast_to(fine_sin[at : at + 1], (8, LANES))
        for piece in range(PIECES):
            spot = (slice(at, at + 1), slice(piece, piece + 1))
            phases[base + 2 + piece] = jnp.broadcast_to(coarse_cos[spot], (8, LANES))
            phases[base + 2 + PIECES + piece] = jnp.broadcast_to(coarse_sin[spot], (8, LANES))

    for plane in range(4):
        wake_t[plane] = jnp.transpose(wake[plane])
    slots[...] = jnp.zeros_like(slots)
    slots[0:2, 0:slot_dev] = others[...]
    slots[2:3, 0:slot_dev] = fill[...].astype(jnp.float32)

    def add_up(step, total):
        for plane in range(2):
            loads(step)[plane].wait()
        at = pl.multiple_of(step * chunk, chunk)
        sums = list(total)
        for piece in range(chunk // LANES):
            where = pl.ds(at + piece * LANES, LANES)
            k = piece % 4
            sums[k] = sums[k] + x_buf[:, where]
            sums[4 + k] = sums[4 + k] + y_buf[:, where]
        return tuple(sums)

    sums = lax.fori_loop(0, chunks, add_up, (zeros,) * 8)
    sum_x = lanes_sum((sums[0] + sums[1]) + (sums[2] + sums[3]))
    sum_y = lanes_sum((sums[4] + sums[5]) + (sums[6] + sums[7]))
    mean = 1.0 / (part_dev * n_dom)
    diagonal = lane == row
    once = jnp.where(me_d == 0, 1.0, 0.0)
    filled = slots[2:3, :]
    tracked = lane[0:1] < bunch_dev
    track_x = rows_sum(jnp.where(diagonal, sum_x, 0.0)) * mean
    track_y = rows_sum(jnp.where(diagonal, sum_y, 0.0)) * mean
    centre_x = filled * jnp.where(tracked, track_x, slots[0:1, :] * once)
    centre_y = filled * jnp.where(tracked, track_y, slots[1:2, :] * once)
    block_own[...] = jnp.where(
        second, lanes_sum(tail_y * centre_y), lanes_sum(tail_x * centre_x)
    )

    pl.semaphore_wait(barrier, n_cycle - 1 + n_dom - 1)

    def block_copy(k):
        return pltpu.make_async_remote_copy(
            src_ref=block_own,
            dst_ref=block_got.at[k],
            send_sem=block_send.at[k],
            recv_sem=block_recv.at[k],
            device_id=cycle_peers[k],
            device_id_type=MESH,
        )

    for k in range(n_cycle - 1):
        block_copy(k).start()

    grid_sum[...] = jnp.zeros_like(grid_sum)
    high_ids = lax.broadcasted_iota(jnp.int32, (HIGH, step_len), 0)
    low_ids = lax.broadcasted_iota(jnp.int32, (LOW, step_len), 0).astype(jnp.bfloat16)
    one, zero = jnp.bfloat16(1), jnp.bfloat16(0)
    shift = LOW.bit_length() - 1

    def deposit(step, _):
        at = pl.multiple_of(step * step_len, step_len)
        where = pl.ds(at, step_len)
        x, y, level = x_buf[:, where], y_buf[:, where], i_buf[:, where]
        x_low = x - x.astype(jnp.bfloat16).astype(jnp.float32)
        y_low = y - y.astype(jnp.bfloat16).astype(jnp.float32)
        high = lax.shift_right_logical(level, shift)
        low = (level & (LOW - 1)).astype(jnp.float32).astype(jnp.bfloat16)
        for b in range(bunch_dev):
            mask = high_ids == high[b : b + 1]
            values = (1.0, x[b : b + 1], y[b : b + 1], x_low[b : b + 1], y_low[b : b + 1])
            left = jnp.concatenate([jnp.where(mask, v, 0.0) for v in values], axis=0)
            right = jnp.where(low_ids == low[b : b + 1], one, zero)
            grid_sum[b] += lax.dot_general(
                left.astype(jnp.bfloat16),
                right,
                (((1,), (1,)), ((), ())),
                preferred_element_type=jnp.float32,
            )
        return 0

    for step in range(chunks):
        loads(step)[2].wait()
    lax.fori_loop(0, part_dev // step_len, deposit, 0)

    for b in range(bunch_dev):
        part = grid_sum[b]
        kinds = (
            part[0:HIGH],
            part[HIGH : 2 * HIGH] + part[3 * HIGH : 4 * HIGH],
            part[2 * HIGH : 3 * HIGH] + part[4 * HIGH : 5 * HIGH],
        )
        for v in range(3):
            for h in range(HIGH):
                at = v * SLICES + h * LOW
                mine[b : b + 1, at : at + LOW] = kinds[v][h : h + 1]

    carried = block_own[...]
    for k in reversed(range(n_cycle - 1)):
        block_copy(k).wait()
        carried = block_decay * carried + block_got[k]
    pieces = ahead * (carried / closing)
    for j in range(bunch_dev - 1):
        centre = jnp.where(second, centre_y[:, j : j + 1], centre_x[:, j : j + 1])
        gap = jnp.maximum(half - 1 - j, 0).astype(jnp.float32)
        inner = coef_both * jnp.exp(-decay_both * gap) * centre
        pieces = pieces + jnp.where(half > j, inner, 0.0)
    long_row = rows_sum(pieces)
    long_at = 3 * SLICES
    mine[:, long_at : long_at + LANES] = jnp.broadcast_to(
        lanes_sum(jnp.where(lane == row, long_row, 0.0)), (8, LANES)
    )
    mine[:, long_at + LANES : long_at + 2 * LANES] = jnp.broadcast_to(
        lanes_sum(jnp.where(lane == row + 64, long_row, 0.0)), (8, LANES)
    )

    def dom_copy(k):
        return pltpu.make_async_remote_copy(
            src_ref=mine,
            dst_ref=theirs.at[k],
            send_sem=dom_send.at[k],
            recv_sem=dom_recv.at[k],
            device_id=dom_peers[k],
            device_id_type=MESH,
        )

    for k in range(n_dom - 1):
        dom_copy(k).start()
    total = mine[...]
    for k in range(n_dom - 1):
        dom_copy(k).wait()
        total = total + theirs[k]

    scale_moment = SLICES / (part_dev * n_dom)
    for v in range(3):
        padded[v, :, 0:LANES] = zeros
        padded[v, :, LANES:] = total[:, v * SLICES : (v + 1) * SLICES] * scale_moment
    kicks = [jnp.zeros((8, SLICES), jnp.float32)] * 4
    for lag in range(BAND):
        count, mom_x, mom_y = (
            padded[v, :, LANES - lag : LANES - lag + SLICES] for v in range(3)
        )
        for c, source in enumerate((mom_x, count, mom_y, count)):
            kicks[c] = kicks[c] + wake_t[c, lag : lag + 1, :] * source
    long_x = total[:, long_at : long_at + 1]
    long_y = total[:, long_at + LANES : long_at + LANES + 1]
    tables[0] = kicks[0] + long_x
    tables[1] = kicks[1]
    tables[2] = kicks[2] + long_y
    tables[3] = kicks[3]


def track_kernel(
    chunk, unroll, coords, index, tables, phases, result, c_buf, i_buf, o_buf, in_sem, out_sem
):
    part_dev = i_buf.shape[1]
    chunks = part_dev // chunk

    def moves(step):
        where = pl.ds(step * chunk, chunk)
        return (
            pltpu.make_async_copy(
                coords.at[:, :, where], c_buf.at[:, :, where], in_sem.at[0, step]
            ),
            pltpu.make_async_copy(index.at[:, where], i_buf.at[:, where], in_sem.at[1, step]),
            pltpu.make_async_copy(
                o_buf.at[:, :, where], result.at[:, :, where], out_sem.at[step]
            ),
        )

    for step in range(chunks):
        load, load_index, _ = moves(step)
        load.start()
        load_index.start()

    def track(step, _):
        where = pl.ds(pl.multiple_of(step * LANES, LANES), LANES)
        level = i_buf[:, where]
        low = level & (LANES - 1)
        piece = lax.shift_right_logical(level, 7)
        odd, upper = (piece & 1) == 1, piece >= 2

        def pick(values):
            return jnp.where(
                upper,
                jnp.where(odd, values[3], values[2]),
                jnp.where(odd, values[1], values[0]),
            )

        def look(table):
            return jnp.take_along_axis(table, low, axis=1)

        def look_up(k):
            return pick(
                [look(tables[k, :, p * LANES : (p + 1) * LANES]) for p in range(PIECES)]
            )

        for plane in range(2):
            base = plane * (2 + 2 * PIECES)
            pos, mom = c_buf[2 * plane, :, where], c_buf[2 * plane + 1, :, where]
            kicked = mom + look_up(2 * plane) + look_up(2 * plane + 1) * pos
            fine_cos, fine_sin = look(phases[base]), look(phases[base + 1])
            coarse_cos = pick([phases[base + 2 + p] for p in range(PIECES)])
            coarse_sin = pick([phases[base + 2 + PIECES + p] for p in range(PIECES)])
            cos = coarse_cos * fine_cos - coarse_sin * fine_sin
            sin = coarse_sin * fine_cos + coarse_cos * fine_sin
            o_buf[2 * plane, :, where] = cos * pos + sin * kicked
            o_buf[2 * plane + 1, :, where] = cos * kicked - sin * pos
        return 0

    each = chunk // LANES
    for step in range(chunks):
        load, load_index, store = moves(step)
        load.wait()
        load_index.wait()
        lax.fori_loop(step * each, (step + 1) * each, track, 0, unroll=unroll)
        store.start()
    for step in range(chunks):
        moves(step)[2].wait()


def on_device(coords, slice_index, fill, others, wake, decay, coef, tunes, chroma):
    _, bunch_dev, part_dev = coords.shape
    n_dom, n_cycle = lax.axis_size("dom"), lax.axis_size("bunch")
    chunk, step_len = 8192, 4096
    chunks = part_dev // chunk
    width = 3 * SLICES + 2 * LANES
    phase_count = 2 * (2 + 2 * PIECES)
    f32 = jnp.float32
    vmem = pl.BlockSpec(memory_space=pltpu.VMEM)
    smem = pl.BlockSpec(memory_space=pltpu.SMEM)
    hbm = pl.BlockSpec(memory_space=pl.ANY)
    dma = pltpu.SemaphoreType.DMA
    tables, phases = pl.pallas_call(
        functools.partial(deposit_kernel, n_cycle, n_dom, chunk, step_len),
        out_shape=(
            jax.ShapeDtypeStruct((4, bunch_dev, SLICES), f32),
            jax.ShapeDtypeStruct((phase_count, 8, LANES), f32),
        ),
        in_specs=[hbm, hbm, vmem, vmem, vmem, smem, smem, smem, smem],
        out_specs=(vmem, vmem),
        scratch_shapes=[
            pltpu.VMEM((bunch_dev, part_dev), f32),
            pltpu.VMEM((bunch_dev, part_dev), f32),
            pltpu.VMEM((bunch_dev, part_dev), jnp.int32),
            pltpu.VMEM((4, BAND, SLICES), f32),
            pltpu.VMEM((bunch_dev, 5 * HIGH, LOW), f32),
            pltpu.VMEM((8, LANES), f32),
            pltpu.VMEM((8, LANES), f32),
            pltpu.VMEM((8, LANES), f32),
            pltpu.VMEM((n_cycle - 1, 8, LANES), f32),
            pltpu.VMEM((bunch_dev, width), f32),
            pltpu.VMEM((n_dom - 1, bunch_dev, width), f32),
            pltpu.VMEM((3, bunch_dev, LANES + SLICES), f32),
            dma((3, chunks)),
            dma((n_cycle - 1,)),
            dma((n_cycle - 1,)),
            dma((n_dom - 1,)),
            dma((n_dom - 1,)),
        ],
        compiler_params=pltpu.CompilerParams(
            collective_id=0, has_side_effects=True, vmem_limit_bytes=40 << 20
        ),
        name="deposit",
    )(coords, slice_index, fill[None], others, wake, decay, coef, tunes, chroma)
    chunk = 4096
    chunks = part_dev // chunk
    return pl.pallas_call(
        functools.partial(track_kernel, chunk, 16),
        out_shape=jax.ShapeDtypeStruct(coords.shape, f32),
        in_specs=[hbm, hbm, vmem, vmem],
        out_specs=hbm,
        scratch_shapes=[
            pltpu.VMEM(coords.shape, f32),
            pltpu.VMEM((bunch_dev, part_dev), jnp.int32),
            pltpu.VMEM(coords.shape, f32),
            dma((2, chunks)),
            dma((chunks,)),
        ],
        compiler_params=pltpu.CompilerParams(vmem_limit_bytes=40 << 20),
        name="track",
    )(coords, slice_index, tables, phases)


def solution(mesh):
    placed = (
        P(None, "bunch", "dom"),
        P("bunch", "dom"),
        P("bunch"),
        P(None, "bunch"),
        P(),
        P(),
        P(),
        P(),
        P(),
    )
    return jax.shard_map(
        on_device, mesh=mesh, in_specs=placed, out_specs=P(None, "bunch", "dom"), check_vma=False
    )
```

```python
import functools
import math

import jax
import jax.numpy as jnp
from jax import lax
from jax.experimental import pallas as pl
from jax.experimental.pallas import tpu as pltpu
from jax.sharding import PartitionSpec as P

SLICES = 512
BAND = 64
LANES = 128
PIECES = SLICES // LANES
LOW = 64
HIGH = SLICES // LOW
MESH = pl.DeviceIdType.MESH


def rows_sum(value):
    return jnp.sum(value, axis=0, keepdims=True)


def lanes_sum(value):
    return jnp.sum(value, axis=1, keepdims=True)


def deposit_kernel(
    n_cycle,
    n_dom,
    chunk,
    step_len,
    coords,
    index,
    fill,
    others,
    wake,
    decay,
    coef,
    tunes,
    chroma,
    tables,
    phases,
    c_buf,
    i_buf,
    fill_v,
    others_v,
    wake_t,
    decay_v,
    coef_v,
    tunes_v,
    chroma_v,
    grid_sum,
    slots,
    outgoing,
    block_own,
    block_got,
    mine,
    theirs,
    padded,
    in_sem,
    small_sem,
    block_send,
    block_recv,
    dom_send,
    dom_recv,
):
    bunch_dev, part_dev = i_buf.shape
    slot_dev = fill.shape[1]
    chunks = part_dev // chunk
    me_b, me_d = lax.axis_index("bunch"), lax.axis_index("dom")

    small = [
        pltpu.make_async_copy(source, target, small_sem.at[k])
        for k, (source, target) in enumerate(
            (
                (tunes, tunes_v),
                (chroma, chroma_v),
                (decay, decay_v),
                (coef, coef_v),
                (fill, fill_v),
                (others, others_v),
                (wake, wake_t),
            )
        )
    ]

    def load(plane, step):
        where = pl.ds(pl.multiple_of(step * chunk, chunk), chunk)
        if plane == 4:
            return pltpu.make_async_copy(
                index.at[:, where], i_buf.at[:, where], in_sem.at[4, step]
            )
        return pltpu.make_async_copy(
            coords.at[plane, :, where], c_buf.at[plane, :, where], in_sem.at[plane, step]
        )

    for copy in small[:-1]:
        copy.start()
    for step in range(chunks):
        load(0, step).start()
        load(2, step).start()
    for plane in (4, 1, 3):
        for step in range(chunks):
            load(plane, step).start()
    small[-1].start()

    cycle_peers = [(lax.rem(me_b + k, n_cycle), me_d) for k in range(1, n_cycle)]
    dom_peers = [(me_b, lax.rem(me_d + k, n_dom)) for k in range(1, n_dom)]
    barrier = pltpu.get_barrier_semaphore()
    for peer in cycle_peers + dom_peers:
        pl.semaphore_signal(barrier, inc=1, device_id=peer, device_id_type=MESH)

    lane = lax.broadcasted_iota(jnp.int32, (8, LANES), 1)
    row = lax.broadcasted_iota(jnp.int32, (8, LANES), 0)
    second = lane >= 64
    half = jnp.where(second, lane - 64, lane)
    half_f = half.astype(jnp.float32)
    zeros = jnp.zeros((8, LANES), jnp.float32)

    for copy in small[:-1]:
        copy.wait()
    slots[...] = jnp.zeros_like(slots)
    slots[0:2, 0:slot_dev] = others_v[...]
    slots[2:3, 0:slot_dev] = fill_v[...].astype(jnp.float32)
    slots[3:5, 0:8] = decay_v[...]
    slots[5:7, 0:8] = coef_v[...]

    def by_row(at):
        return lanes_sum(jnp.where(lane == row, slots[at : at + 1, :], 0.0))

    decay_x, decay_y = by_row(3), by_row(4)
    decay_both = jnp.where(second, decay_y, decay_x)
    coef_both = jnp.where(second, by_row(6), by_row(5))
    back = (slot_dev - 1 - lane).astype(jnp.float32)
    inside = lane < slot_dev
    back = jnp.where(inside, back, 0.0)
    tail_x = jnp.where(inside, jnp.exp(-decay_x * back), 0.0)
    tail_y = jnp.where(inside, jnp.exp(-decay_y * back), 0.0)
    block_decay = jnp.exp(-decay_both * slot_dev)
    closing = 1.0 - jnp.exp(-decay_both * (slot_dev * n_cycle))
    ahead = coef_both * jnp.exp(-decay_both * half_f)

    lower = row < 4
    chroma_rows = jnp.where(lower, chroma_v[:, 0:1], chroma_v[:, 1:2])
    tune_rows = jnp.where(lower, tunes_v[:, 0:1], tunes_v[:, 1:2])
    fine = chroma_rows * (lane.astype(jnp.float32) * (2.0 / SLICES))
    first = 2.0 * ((lane & 3).astype(jnp.float32) * LANES + 0.5) / SLICES - 1.0
    coarse = 2.0 * math.pi * tune_rows + chroma_rows * first
    fine_cos, fine_sin = jnp.cos(fine), jnp.sin(fine)
    coarse_cos, coarse_sin = jnp.cos(coarse), jnp.sin(coarse)
    for plane in range(2):
        at = 4 * plane
        base = plane * (2 + 2 * PIECES)
        phases[base] = jnp.broadcast_to(fine_cos[at : at + 1], (8, LANES))
        phases[base + 1] = jnp.broadcast_to(fine_sin[at : at + 1], (8, LANES))
        for piece in range(PIECES):
            spot = (slice(at, at + 1), slice(piece, piece + 1))
            phases[base + 2 + piece] = jnp.broadcast_to(coarse_cos[spot], (8, LANES))
            phases[base + 2 + PIECES + piece] = jnp.broadcast_to(coarse_sin[spot], (8, LANES))

    def add_up(step, total):
        load(0, step).wait()
        load(2, step).wait()
        at = pl.multiple_of(step * chunk, chunk)
        sums = list(total)
        for piece in range(chunk // LANES):
            where = pl.ds(at + piece * LANES, LANES)
            k = piece % 4
            sums[k] = sums[k] + c_buf[0, :, where]
            sums[4 + k] = sums[4 + k] + c_buf[2, :, where]
        return tuple(sums)

    sums = lax.fori_loop(0, chunks, add_up, (zeros,) * 8)
    sum_x = lanes_sum((sums[0] + sums[1]) + (sums[2] + sums[3]))
    sum_y = lanes_sum((sums[4] + sums[5]) + (sums[6] + sums[7]))
    mean = 1.0 / (part_dev * n_dom)
    diagonal = lane == row
    once = jnp.where(me_d == 0, 1.0, 0.0)
    filled = slots[2:3, :]
    tracked = lane[0:1] < bunch_dev
    track_x = rows_sum(jnp.where(diagonal, sum_x, 0.0)) * mean
    track_y = rows_sum(jnp.where(diagonal, sum_y, 0.0)) * mean
    centre_x = filled * jnp.where(tracked, track_x, slots[0:1, :] * once)
    centre_y = filled * jnp.where(tracked, track_y, slots[1:2, :] * once)
    block_own[...] = jnp.where(
        second, lanes_sum(tail_y * centre_y), lanes_sum(tail_x * centre_x)
    )

    pl.semaphore_wait(barrier, n_cycle - 1 + n_dom - 1)

    def block_copy(k):
        return pltpu.make_async_remote_copy(
            src_ref=block_own,
            dst_ref=block_got.at[k],
            send_sem=block_send.at[k],
            recv_sem=block_recv.at[k],
            device_id=cycle_peers[k],
            device_id_type=MESH,
        )

    for k in range(n_cycle - 1):
        block_copy(k).start()

    grid_sum[...] = jnp.zeros_like(grid_sum)
    high_ids = lax.broadcasted_iota(jnp.int32, (HIGH, step_len), 0)
    low_ids = lax.broadcasted_iota(jnp.int32, (LOW, step_len), 0).astype(jnp.bfloat16)
    one, zero = jnp.bfloat16(1), jnp.bfloat16(0)
    shift = LOW.bit_length() - 1

    def deposit(step, _):
        at = pl.multiple_of(step * step_len, step_len)
        where = pl.ds(at, step_len)
        x, y, level = c_buf[0, :, where], c_buf[2, :, where], i_buf[:, where]
        x_low = x - x.astype(jnp.bfloat16).astype(jnp.float32)
        y_low = y - y.astype(jnp.bfloat16).astype(jnp.float32)
        high = lax.shift_right_logical(level, shift)
        low = (level & (LOW - 1)).astype(jnp.float32).astype(jnp.bfloat16)
        for b in range(bunch_dev):
            mask = high_ids == high[b : b + 1]
            values = (1.0, x[b : b + 1], y[b : b + 1], x_low[b : b + 1], y_low[b : b + 1])
            left = jnp.concatenate([jnp.where(mask, v, 0.0) for v in values], axis=0)
            right = jnp.where(low_ids == low[b : b + 1], one, zero)
            grid_sum[b] += lax.dot_general(
                left.astype(jnp.bfloat16),
                right,
                (((1,), (1,)), ((), ())),
                preferred_element_type=jnp.float32,
            )
        return 0

    for step in range(chunks):
        load(4, step).wait()
    lax.fori_loop(0, part_dev // step_len, deposit, 0)

    for b in range(bunch_dev):
        part = grid_sum[b]
        kinds = (
            part[0:HIGH],
            part[HIGH : 2 * HIGH] + part[3 * HIGH : 4 * HIGH],
            part[2 * HIGH : 3 * HIGH] + part[4 * HIGH : 5 * HIGH],
        )
        for v in range(3):
            for h in range(HIGH):
                at = v * SLICES + h * LOW
                mine[b : b + 1, at : at + LOW] = kinds[v][h : h + 1]

    carried = block_own[...]
    for k in reversed(range(n_cycle - 1)):
        block_copy(k).wait()
        carried = block_decay * carried + block_got[k]
    pieces = ahead * (carried / closing)
    for j in range(bunch_dev - 1):
        centre = jnp.where(second, centre_y[:, j : j + 1], centre_x[:, j : j + 1])
        gap = jnp.maximum(half - 1 - j, 0).astype(jnp.float32)
        inner = coef_both * jnp.exp(-decay_both * gap) * centre
        pieces = pieces + jnp.where(half > j, inner, 0.0)
    long_row = rows_sum(pieces)
    long_at = 3 * SLICES
    mine[:, long_at : long_at + LANES] = jnp.broadcast_to(
        lanes_sum(jnp.where(lane == row, long_row, 0.0)), (8, LANES)
    )
    mine[:, long_at + LANES : long_at + 2 * LANES] = jnp.broadcast_to(
        lanes_sum(jnp.where(lane == row + 64, long_row, 0.0)), (8, LANES)
    )

    def dom_copy(k):
        return pltpu.make_async_remote_copy(
            src_ref=mine,
            dst_ref=theirs.at[k],
            send_sem=dom_send.at[k],
            recv_sem=dom_recv.at[k],
            device_id=dom_peers[k],
            device_id_type=MESH,
        )

    for k in range(n_dom - 1):
        dom_copy(k).start()
    total = mine[...]
    for k in range(n_dom - 1):
        dom_copy(k).wait()
        total = total + theirs[k]

    small[-1].wait()
    for plane in (1, 3):
        for step in range(chunks):
            load(plane, step).wait()
    scale_moment = SLICES / (part_dev * n_dom)
    for v in range(3):
        padded[v, :, 0:LANES] = zeros
        padded[v, :, LANES:] = total[:, v * SLICES : (v + 1) * SLICES] * scale_moment
    kicks = [jnp.zeros((8, SLICES), jnp.float32)] * 4
    for lag in range(BAND):
        count, mom_x, mom_y = (
            padded[v, :, LANES - lag : LANES - lag + SLICES] for v in range(3)
        )
        for c, source in enumerate((mom_x, count, mom_y, count)):
            kicks[c] = kicks[c] + wake_t[c, lag : lag + 1, :] * source
    long_x = total[:, long_at : long_at + 1]
    long_y = total[:, long_at + LANES : long_at + LANES + 1]
    tables[0] = kicks[0] + long_x
    tables[1] = kicks[1]
    tables[2] = kicks[2] + long_y
    tables[3] = kicks[3]


def track_kernel(chunk, unroll, c_buf, i_buf, tables, phases, result, o_buf, out_sem):
    part_dev = i_buf.shape[1]
    chunks = part_dev // chunk

    def store(step):
        where = pl.ds(step * chunk, chunk)
        return pltpu.make_async_copy(
            o_buf.at[:, :, where], result.at[:, :, where], out_sem.at[step]
        )

    def track(step, _):
        where = pl.ds(pl.multiple_of(step * LANES, LANES), LANES)
        level = i_buf[:, where]
        low = level & (LANES - 1)
        piece = lax.shift_right_logical(level, 7)
        odd, upper = (piece & 1) == 1, piece >= 2

        def pick(values):
            return jnp.where(
                upper,
                jnp.where(odd, values[3], values[2]),
                jnp.where(odd, values[1], values[0]),
            )

        def look(table):
            return jnp.take_along_axis(table, low, axis=1)

        def look_up(k):
            return pick(
                [look(tables[k, :, p * LANES : (p + 1) * LANES]) for p in range(PIECES)]
            )

        for plane in range(2):
            base = plane * (2 + 2 * PIECES)
            pos, mom = c_buf[2 * plane, :, where], c_buf[2 * plane + 1, :, where]
            kicked = mom + look_up(2 * plane) + look_up(2 * plane + 1) * pos
            fine_cos, fine_sin = look(phases[base]), look(phases[base + 1])
            coarse_cos = pick([phases[base + 2 + p] for p in range(PIECES)])
            coarse_sin = pick([phases[base + 2 + PIECES + p] for p in range(PIECES)])
            cos = coarse_cos * fine_cos - coarse_sin * fine_sin
            sin = coarse_sin * fine_cos + coarse_cos * fine_sin
            o_buf[2 * plane, :, where] = cos * pos + sin * kicked
            o_buf[2 * plane + 1, :, where] = cos * kicked - sin * pos
        return 0

    each = chunk // LANES
    for step in range(chunks):
        lax.fori_loop(step * each, (step + 1) * each, track, 0, unroll=unroll)
        store(step).start()
    for step in range(chunks):
        store(step).wait()


def on_device(coords, slice_index, fill, others, wake, decay, coef, tunes, chroma):
    hold = lambda a: pltpu.with_memory_space_constraint(a, pltpu.HBM)
    _, bunch_dev, part_dev = coords.shape
    n_dom, n_cycle = lax.axis_size("dom"), lax.axis_size("bunch")
    chunk, step_len = 8192, 8192
    chunks = part_dev // chunk
    width = 3 * SLICES + 2 * LANES
    phase_count = 2 * (2 + 2 * PIECES)
    f32 = jnp.float32
    vmem = pl.BlockSpec(memory_space=pltpu.VMEM)
    hbm = pl.BlockSpec(memory_space=pltpu.HBM)
    dma = pltpu.SemaphoreType.DMA
    tables, phases, held, held_index = pl.pallas_call(
        functools.partial(deposit_kernel, n_cycle, n_dom, chunk, step_len),
        out_shape=(
            jax.ShapeDtypeStruct((4, bunch_dev, SLICES), f32),
            jax.ShapeDtypeStruct((phase_count, 8, LANES), f32),
            jax.ShapeDtypeStruct(coords.shape, f32),
            jax.ShapeDtypeStruct((bunch_dev, part_dev), jnp.int32),
        ),
        in_specs=[hbm] * 9,
        out_specs=(vmem,) * 4,
        scratch_shapes=[
            pltpu.VMEM((1, fill.shape[0]), jnp.int32),
            pltpu.VMEM(others.shape, f32),
            pltpu.VMEM((4, BAND, SLICES), f32),
            pltpu.VMEM(decay.shape, f32),
            pltpu.VMEM(coef.shape, f32),
            pltpu.VMEM((1, 2), f32),
            pltpu.VMEM((1, 2), f32),
            pltpu.VMEM((bunch_dev, 5 * HIGH, LOW), f32),
            pltpu.VMEM((8, LANES), f32),
            pltpu.VMEM((8, LANES), f32),
            pltpu.VMEM((8, LANES), f32),
            pltpu.VMEM((n_cycle - 1, 8, LANES), f32),
            pltpu.VMEM((bunch_dev, width), f32),
            pltpu.VMEM((n_dom - 1, bunch_dev, width), f32),
            pltpu.VMEM((3, bunch_dev, LANES + SLICES), f32),
            dma((5, chunks)),
            dma((7,)),
            dma((n_cycle - 1,)),
            dma((n_cycle - 1,)),
            dma((n_dom - 1,)),
            dma((n_dom - 1,)),
        ],
        compiler_params=pltpu.CompilerParams(
            collective_id=0, has_side_effects=True, vmem_limit_bytes=40 << 20
        ),
        name="deposit",
    )(
        *(
            hold(a)
            for a in (
                coords,
                slice_index,
                fill[None],
                others,
                jnp.swapaxes(wake, 1, 2),
                decay,
                coef,
                tunes[None],
                chroma[None],
            )
        )
    )
    chunk = 4096
    chunks = part_dev // chunk
    return pl.pallas_call(
        functools.partial(track_kernel, chunk, 16),
        out_shape=jax.ShapeDtypeStruct(coords.shape, f32),
        in_specs=[vmem] * 4,
        out_specs=hbm,
        scratch_shapes=[pltpu.VMEM(coords.shape, f32), dma((chunks,))],
        compiler_params=pltpu.CompilerParams(vmem_limit_bytes=40 << 20),
        name="track",
    )(held, held_index, tables, phases)


def solution(mesh):
    placed = (
        P(None, "bunch", "dom"),
        P("bunch", "dom"),
        P("bunch"),
        P(None, "bunch"),
        P(),
        P(),
        P(),
        P(),
        P(),
    )
    return jax.shard_map(
        on_device, mesh=mesh, in_specs=placed, out_specs=P(None, "bunch", "dom"), check_vma=False
    )
```

```python
import functools
import math

import jax
import jax.numpy as jnp
from jax import lax
from jax.experimental import pallas as pl
from jax.experimental.pallas import tpu as pltpu
from jax.sharding import PartitionSpec as P

SLICES = 512
BAND = 64
LANES = 128
PIECES = SLICES // LANES
LOW = 64
HIGH = SLICES // LOW
MESH = pl.DeviceIdType.MESH


def rows_sum(value):
    return jnp.sum(value, axis=0, keepdims=True)


def lanes_sum(value):
    return jnp.sum(value, axis=1, keepdims=True)


def deposit_kernel(
    n_cycle,
    n_dom,
    chunk,
    step_len,
    coords,
    index,
    fill,
    others,
    wake,
    decay,
    coef,
    tunes,
    chroma,
    tables,
    phases,
    c_buf,
    i_buf,
    fill_v,
    others_v,
    wake_t,
    decay_v,
    coef_v,
    tunes_v,
    chroma_v,
    grid_sum,
    slots,
    outgoing,
    block_own,
    block_got,
    mine,
    theirs,
    padded,
    in_sem,
    small_sem,
    block_send,
    block_recv,
    dom_send,
    dom_recv,
):
    bunch_dev, part_dev = i_buf.shape
    slot_dev = fill.shape[1]
    chunks = part_dev // chunk
    me_b, me_d = lax.axis_index("bunch"), lax.axis_index("dom")

    small = [
        pltpu.make_async_copy(source, target, small_sem.at[k])
        for k, (source, target) in enumerate(
            (
                (tunes, tunes_v),
                (chroma, chroma_v),
                (decay, decay_v),
                (coef, coef_v),
                (fill, fill_v),
                (others, others_v),
                (wake, wake_t),
            )
        )
    ]

    def load(plane, step):
        where = pl.ds(pl.multiple_of(step * chunk, chunk), chunk)
        if plane == 4:
            return pltpu.make_async_copy(
                index.at[:, where], i_buf.at[:, where], in_sem.at[4, step]
            )
        return pltpu.make_async_copy(
            coords.at[plane, :, where], c_buf.at[plane, :, where], in_sem.at[plane, step]
        )

    for copy in small[:-1]:
        copy.start()
    for step in range(chunks):
        load(0, step).start()
        load(2, step).start()
        load(4, step).start()
    for plane in (1, 3):
        for step in range(chunks):
            load(plane, step).start()
    small[-1].start()

    cycle_peers = [(lax.rem(me_b + k, n_cycle), me_d) for k in range(1, n_cycle)]
    dom_peers = [(me_b, lax.rem(me_d + k, n_dom)) for k in range(1, n_dom)]
    barrier = pltpu.get_barrier_semaphore()
    for peer in cycle_peers + dom_peers:
        pl.semaphore_signal(barrier, inc=1, device_id=peer, device_id_type=MESH)

    lane = lax.broadcasted_iota(jnp.int32, (8, LANES), 1)
    row = lax.broadcasted_iota(jnp.int32, (8, LANES), 0)
    second = lane >= 64
    half = jnp.where(second, lane - 64, lane)
    half_f = half.astype(jnp.float32)
    zeros = jnp.zeros((8, LANES), jnp.float32)

    for copy in small[:-1]:
        copy.wait()
    slots[...] = jnp.zeros_like(slots)
    slots[0:2, 0:slot_dev] = others_v[...]
    slots[2:3, 0:slot_dev] = fill_v[...].astype(jnp.float32)
    slots[3:5, 0:8] = decay_v[...]
    slots[5:7, 0:8] = coef_v[...]

    def by_row(at):
        return lanes_sum(jnp.where(lane == row, slots[at : at + 1, :], 0.0))

    decay_x, decay_y = by_row(3), by_row(4)
    decay_both = jnp.where(second, decay_y, decay_x)
    coef_both = jnp.where(second, by_row(6), by_row(5))
    back = (slot_dev - 1 - lane).astype(jnp.float32)
    inside = lane < slot_dev
    back = jnp.where(inside, back, 0.0)
    tail_x = jnp.where(inside, jnp.exp(-decay_x * back), 0.0)
    tail_y = jnp.where(inside, jnp.exp(-decay_y * back), 0.0)
    block_decay = jnp.exp(-decay_both * slot_dev)
    closing = 1.0 - jnp.exp(-decay_both * (slot_dev * n_cycle))
    ahead = coef_both * jnp.exp(-decay_both * half_f)

    lower = row < 4
    chroma_rows = jnp.where(lower, chroma_v[:, 0:1], chroma_v[:, 1:2])
    tune_rows = jnp.where(lower, tunes_v[:, 0:1], tunes_v[:, 1:2])
    fine = chroma_rows * (lane.astype(jnp.float32) * (2.0 / SLICES))
    first = 2.0 * ((lane & 3).astype(jnp.float32) * LANES + 0.5) / SLICES - 1.0
    coarse = 2.0 * math.pi * tune_rows + chroma_rows * first
    fine_cos, fine_sin = jnp.cos(fine), jnp.sin(fine)
    coarse_cos, coarse_sin = jnp.cos(coarse), jnp.sin(coarse)
    for plane in range(2):
        at = 4 * plane
        base = plane * (2 + 2 * PIECES)
        phases[base] = jnp.broadcast_to(fine_cos[at : at + 1], (8, LANES))
        phases[base + 1] = jnp.broadcast_to(fine_sin[at : at + 1], (8, LANES))
        for piece in range(PIECES):
            spot = (slice(at, at + 1), slice(piece, piece + 1))
            phases[base + 2 + piece] = jnp.broadcast_to(coarse_cos[spot], (8, LANES))
            phases[base + 2 + PIECES + piece] = jnp.broadcast_to(coarse_sin[spot], (8, LANES))

    grid_sum[...] = jnp.zeros_like(grid_sum)
    high_ids = lax.broadcasted_iota(jnp.int32, (HIGH, step_len), 0)
    low_ids = lax.broadcasted_iota(jnp.int32, (LOW, step_len), 0).astype(jnp.bfloat16)
    one, zero = jnp.bfloat16(1), jnp.bfloat16(0)
    shift = LOW.bit_length() - 1

    def deposit(step, _):
        at = pl.multiple_of(step * step_len, step_len)
        where = pl.ds(at, step_len)
        x, y, level = c_buf[0, :, where], c_buf[2, :, where], i_buf[:, where]
        x_low = x - x.astype(jnp.bfloat16).astype(jnp.float32)
        y_low = y - y.astype(jnp.bfloat16).astype(jnp.float32)
        high = lax.shift_right_logical(level, shift)
        low = (level & (LOW - 1)).astype(jnp.float32).astype(jnp.bfloat16)
        for b in range(bunch_dev):
            mask = high_ids == high[b : b + 1]
            values = (1.0, x[b : b + 1], y[b : b + 1], x_low[b : b + 1], y_low[b : b + 1])
            left = jnp.concatenate([jnp.where(mask, v, 0.0) for v in values], axis=0)
            right = jnp.where(low_ids == low[b : b + 1], one, zero)
            grid_sum[b] += lax.dot_general(
                left.astype(jnp.bfloat16),
                right,
                (((1,), (1,)), ((), ())),
                preferred_element_type=jnp.float32,
            )
        return 0

    for plane in (0, 2, 4):
        load(plane, 0).wait()
    lax.fori_loop(0, chunk // step_len, deposit, 0)

    for step in range(1, chunks):
        load(0, step).wait()
        load(2, step).wait()

    def add_up(step, total):
        at = pl.multiple_of(step * chunk, chunk)
        sums = list(total)
        for piece in range(chunk // LANES):
            where = pl.ds(at + piece * LANES, LANES)
            k = piece % 4
            sums[k] = sums[k] + c_buf[0, :, where]
            sums[4 + k] = sums[4 + k] + c_buf[2, :, where]
        return tuple(sums)

    sums = lax.fori_loop(0, chunks, add_up, (zeros,) * 8)
    sum_x = lanes_sum((sums[0] + sums[1]) + (sums[2] + sums[3]))
    sum_y = lanes_sum((sums[4] + sums[5]) + (sums[6] + sums[7]))
    mean = 1.0 / (part_dev * n_dom)
    diagonal = lane == row
    once = jnp.where(me_d == 0, 1.0, 0.0)
    filled = slots[2:3, :]
    tracked = lane[0:1] < bunch_dev
    track_x = rows_sum(jnp.where(diagonal, sum_x, 0.0)) * mean
    track_y = rows_sum(jnp.where(diagonal, sum_y, 0.0)) * mean
    centre_x = filled * jnp.where(tracked, track_x, slots[0:1, :] * once)
    centre_y = filled * jnp.where(tracked, track_y, slots[1:2, :] * once)
    block_own[...] = jnp.where(
        second, lanes_sum(tail_y * centre_y), lanes_sum(tail_x * centre_x)
    )

    pl.semaphore_wait(barrier, n_cycle - 1 + n_dom - 1)

    def block_copy(k):
        return pltpu.make_async_remote_copy(
            src_ref=block_own,
            dst_ref=block_got.at[k],
            send_sem=block_send.at[k],
            recv_sem=block_recv.at[k],
            device_id=cycle_peers[k],
            device_id_type=MESH,
        )

    for k in range(n_cycle - 1):
        block_copy(k).start()

    for step in range(1, chunks):
        load(4, step).wait()
    lax.fori_loop(chunk // step_len, part_dev // step_len, deposit, 0)

    for b in range(bunch_dev):
        part = grid_sum[b]
        kinds = (
            part[0:HIGH],
            part[HIGH : 2 * HIGH] + part[3 * HIGH : 4 * HIGH],
            part[2 * HIGH : 3 * HIGH] + part[4 * HIGH : 5 * HIGH],
        )
        for v in range(3):
            for h in range(HIGH):
                at = v * SLICES + h * LOW
                mine[b : b + 1, at : at + LOW] = kinds[v][h : h + 1]

    carried = block_own[...]
    for k in reversed(range(n_cycle - 1)):
        block_copy(k).wait()
        carried = block_decay * carried + block_got[k]
    pieces = ahead * (carried / closing)
    for j in range(bunch_dev - 1):
        centre = jnp.where(second, centre_y[:, j : j + 1], centre_x[:, j : j + 1])
        gap = jnp.maximum(half - 1 - j, 0).astype(jnp.float32)
        inner = coef_both * jnp.exp(-decay_both * gap) * centre
        pieces = pieces + jnp.where(half > j, inner, 0.0)
    long_row = rows_sum(pieces)
    long_at = 3 * SLICES
    mine[:, long_at : long_at + LANES] = jnp.broadcast_to(
        lanes_sum(jnp.where(lane == row, long_row, 0.0)), (8, LANES)
    )
    mine[:, long_at + LANES : long_at + 2 * LANES] = jnp.broadcast_to(
        lanes_sum(jnp.where(lane == row + 64, long_row, 0.0)), (8, LANES)
    )

    def dom_copy(k):
        return pltpu.make_async_remote_copy(
            src_ref=mine,
            dst_ref=theirs.at[k],
            send_sem=dom_send.at[k],
            recv_sem=dom_recv.at[k],
            device_id=dom_peers[k],
            device_id_type=MESH,
        )

    for k in range(n_dom - 1):
        dom_copy(k).start()
    total = mine[...]
    for k in range(n_dom - 1):
        dom_copy(k).wait()
        total = total + theirs[k]

    small[-1].wait()
    for plane in (1, 3):
        for step in range(chunks):
            load(plane, step).wait()
    scale_moment = SLICES / (part_dev * n_dom)
    for v in range(3):
        padded[v, :, 0:LANES] = zeros
        padded[v, :, LANES:] = total[:, v * SLICES : (v + 1) * SLICES] * scale_moment
    kicks = [jnp.zeros((8, SLICES), jnp.float32)] * 4
    for lag in range(BAND):
        count, mom_x, mom_y = (
            padded[v, :, LANES - lag : LANES - lag + SLICES] for v in range(3)
        )
        for c, source in enumerate((mom_x, count, mom_y, count)):
            kicks[c] = kicks[c] + wake_t[c, lag : lag + 1, :] * source
    long_x = total[:, long_at : long_at + 1]
    long_y = total[:, long_at + LANES : long_at + LANES + 1]
    tables[0] = kicks[0] + long_x
    tables[1] = kicks[1]
    tables[2] = kicks[2] + long_y
    tables[3] = kicks[3]


def track_kernel(chunk, unroll, c_buf, i_buf, tables, phases, result, o_buf, out_sem):
    part_dev = i_buf.shape[1]
    chunks = part_dev // chunk

    def store(step):
        where = pl.ds(pl.multiple_of(step * chunk, chunk), chunk)
        return pltpu.make_async_copy(
            o_buf.at[:, :, where], result.at[:, :, where], out_sem.at[step]
        )

    def track(step, _):
        where = pl.ds(pl.multiple_of(step * LANES, LANES), LANES)
        level = i_buf[:, where]
        low = level & (LANES - 1)
        piece = lax.shift_right_logical(level, 7)
        odd, upper = (piece & 1) == 1, piece >= 2

        def pick(values):
            return jnp.where(
                upper,
                jnp.where(odd, values[3], values[2]),
                jnp.where(odd, values[1], values[0]),
            )

        def look(table):
            return jnp.take_along_axis(table, low, axis=1)

        def look_up(k):
            return pick(
                [look(tables[k, :, p * LANES : (p + 1) * LANES]) for p in range(PIECES)]
            )

        for plane in range(2):
            base = plane * (2 + 2 * PIECES)
            pos, mom = c_buf[2 * plane, :, where], c_buf[2 * plane + 1, :, where]
            kicked = mom + look_up(2 * plane) + look_up(2 * plane + 1) * pos
            fine_cos, fine_sin = look(phases[base]), look(phases[base + 1])
            coarse_cos = pick([phases[base + 2 + p] for p in range(PIECES)])
            coarse_sin = pick([phases[base + 2 + PIECES + p] for p in range(PIECES)])
            cos = coarse_cos * fine_cos - coarse_sin * fine_sin
            sin = coarse_sin * fine_cos + coarse_cos * fine_sin
            o_buf[2 * plane, :, where] = cos * pos + sin * kicked
            o_buf[2 * plane + 1, :, where] = cos * kicked - sin * pos
        return 0

    each = chunk // LANES
    def run(step, _):
        lax.fori_loop(0, each, lambda k, z: track(step * each + k, z), 0, unroll=unroll)
        store(step).start()
        return 0

    lax.fori_loop(0, chunks, run, 0)
    for step in range(chunks):
        store(step).wait()


def on_device(coords, slice_index, fill, others, wake, decay, coef, tunes, chroma):
    hold = lambda a: pltpu.with_memory_space_constraint(a, pltpu.HBM)
    _, bunch_dev, part_dev = coords.shape
    n_dom, n_cycle = lax.axis_size("dom"), lax.axis_size("bunch")
    chunk, step_len = 8192, 8192
    chunks = part_dev // chunk
    width = 3 * SLICES + 2 * LANES
    phase_count = 2 * (2 + 2 * PIECES)
    f32 = jnp.float32
    vmem = pl.BlockSpec(memory_space=pltpu.VMEM)
    hbm = pl.BlockSpec(memory_space=pltpu.HBM)
    dma = pltpu.SemaphoreType.DMA
    tables, phases, held, held_index = pl.pallas_call(
        functools.partial(deposit_kernel, n_cycle, n_dom, chunk, step_len),
        out_shape=(
            jax.ShapeDtypeStruct((4, bunch_dev, SLICES), f32),
            jax.ShapeDtypeStruct((phase_count, 8, LANES), f32),
            jax.ShapeDtypeStruct(coords.shape, f32),
            jax.ShapeDtypeStruct((bunch_dev, part_dev), jnp.int32),
        ),
        in_specs=[hbm] * 9,
        out_specs=(vmem,) * 4,
        scratch_shapes=[
            pltpu.VMEM((1, fill.shape[0]), jnp.int32),
            pltpu.VMEM(others.shape, f32),
            pltpu.VMEM((4, BAND, SLICES), f32),
            pltpu.VMEM(decay.shape, f32),
            pltpu.VMEM(coef.shape, f32),
            pltpu.VMEM((1, 2), f32),
            pltpu.VMEM((1, 2), f32),
            pltpu.VMEM((bunch_dev, 5 * HIGH, LOW), f32),
            pltpu.VMEM((8, LANES), f32),
            pltpu.VMEM((8, LANES), f32),
            pltpu.VMEM((8, LANES), f32),
            pltpu.VMEM((n_cycle - 1, 8, LANES), f32),
            pltpu.VMEM((bunch_dev, width), f32),
            pltpu.VMEM((n_dom - 1, bunch_dev, width), f32),
            pltpu.VMEM((3, bunch_dev, LANES + SLICES), f32),
            dma((5, chunks)),
            dma((7,)),
            dma((n_cycle - 1,)),
            dma((n_cycle - 1,)),
            dma((n_dom - 1,)),
            dma((n_dom - 1,)),
        ],
        compiler_params=pltpu.CompilerParams(
            collective_id=0, has_side_effects=True, vmem_limit_bytes=40 << 20
        ),
        name="deposit",
    )(
        *(
            hold(a)
            for a in (
                coords,
                slice_index,
                fill[None],
                others,
                jnp.swapaxes(wake, 1, 2),
                decay,
                coef,
                tunes[None],
                chroma[None],
            )
        )
    )
    chunk = 4096
    chunks = part_dev // chunk
    return pl.pallas_call(
        functools.partial(track_kernel, chunk, 32),
        out_shape=jax.ShapeDtypeStruct(coords.shape, f32),
        in_specs=[vmem] * 4,
        out_specs=hbm,
        scratch_shapes=[pltpu.VMEM(coords.shape, f32), dma((chunks,))],
        compiler_params=pltpu.CompilerParams(vmem_limit_bytes=40 << 20),
        name="track",
    )(held, held_index, tables, phases)


def solution(mesh):
    placed = (
        P(None, "bunch", "dom"),
        P("bunch", "dom"),
        P("bunch"),
        P(None, "bunch"),
        P(),
        P(),
        P(),
        P(),
        P(),
    )
    return jax.shard_map(
        on_device, mesh=mesh, in_specs=placed, out_specs=P(None, "bunch", "dom"), check_vma=False
    )
```

```python
import functools
import math

import jax
import jax.numpy as jnp
from jax import lax
from jax.experimental import pallas as pl
from jax.experimental.pallas import tpu as pltpu
from jax.sharding import PartitionSpec as P

SLICES = 512
BAND = 64
LANES = 128
PIECES = SLICES // LANES
LOW = 64
HIGH = SLICES // LOW
MESH = pl.DeviceIdType.MESH


def rows_sum(value):
    return jnp.sum(value, axis=0, keepdims=True)


def lanes_sum(value):
    return jnp.sum(value, axis=1, keepdims=True)


def deposit_kernel(
    n_cycle,
    n_dom,
    chunk,
    step_len,
    coords,
    index,
    fill,
    others,
    wake,
    decay,
    coef,
    tunes,
    chroma,
    tables,
    phases,
    c_buf,
    i_buf,
    fill_v,
    others_v,
    wake_t,
    decay_v,
    coef_v,
    tunes_v,
    chroma_v,
    grid_sum,
    slots,
    outgoing,
    block_own,
    block_got,
    mine,
    theirs,
    long_mine,
    long_theirs,
    padded,
    in_sem,
    small_sem,
    block_send,
    block_recv,
    dom_send,
    dom_recv,
):
    bunch_dev, part_dev = i_buf.shape
    slot_dev = fill.shape[1]
    chunks = part_dev // chunk
    me_b, me_d = lax.axis_index("bunch"), lax.axis_index("dom")

    small = [
        pltpu.make_async_copy(source, target, small_sem.at[k])
        for k, (source, target) in enumerate(
            (
                (tunes, tunes_v),
                (chroma, chroma_v),
                (decay, decay_v),
                (coef, coef_v),
                (fill, fill_v),
                (others, others_v),
                (wake, wake_t),
            )
        )
    ]

    def load(plane, step):
        where = pl.ds(pl.multiple_of(step * chunk, chunk), chunk)
        if plane == 4:
            return pltpu.make_async_copy(
                index.at[:, where], i_buf.at[:, where], in_sem.at[4, step]
            )
        return pltpu.make_async_copy(
            coords.at[plane, :, where], c_buf.at[plane, :, where], in_sem.at[plane, step]
        )

    for copy in small[:-1]:
        copy.start()
    for step in range(chunks):
        load(0, step).start()
        load(2, step).start()
        load(4, step).start()
    for plane in (1, 3):
        for step in range(chunks):
            load(plane, step).start()
    small[-1].start()

    cycle_peers = [(lax.rem(me_b + k, n_cycle), me_d) for k in range(1, n_cycle)]
    dom_peers = [(me_b, lax.rem(me_d + k, n_dom)) for k in range(1, n_dom)]
    barrier = pltpu.get_barrier_semaphore()
    for peer in cycle_peers + dom_peers:
        pl.semaphore_signal(barrier, inc=1, device_id=peer, device_id_type=MESH)

    lane = lax.broadcasted_iota(jnp.int32, (8, LANES), 1)
    row = lax.broadcasted_iota(jnp.int32, (8, LANES), 0)
    second = lane >= 64
    half = jnp.where(second, lane - 64, lane)
    half_f = half.astype(jnp.float32)
    zeros = jnp.zeros((8, LANES), jnp.float32)

    for copy in small[:-1]:
        copy.wait()
    slots[...] = jnp.zeros_like(slots)
    slots[0:2, 0:slot_dev] = others_v[...]
    slots[2:3, 0:slot_dev] = fill_v[...].astype(jnp.float32)
    slots[3:5, 0:8] = decay_v[...]
    slots[5:7, 0:8] = coef_v[...]

    def by_row(at):
        return lanes_sum(jnp.where(lane == row, slots[at : at + 1, :], 0.0))

    decay_x, decay_y = by_row(3), by_row(4)
    decay_both = jnp.where(second, decay_y, decay_x)
    coef_both = jnp.where(second, by_row(6), by_row(5))
    back = (slot_dev - 1 - lane).astype(jnp.float32)
    inside = lane < slot_dev
    back = jnp.where(inside, back, 0.0)
    tail_x = jnp.where(inside, jnp.exp(-decay_x * back), 0.0)
    tail_y = jnp.where(inside, jnp.exp(-decay_y * back), 0.0)
    block_decay = jnp.exp(-decay_both * slot_dev)
    closing = 1.0 - jnp.exp(-decay_both * (slot_dev * n_cycle))
    ahead = coef_both * jnp.exp(-decay_both * half_f)

    lower = row < 4
    chroma_rows = jnp.where(lower, chroma_v[:, 0:1], chroma_v[:, 1:2])
    tune_rows = jnp.where(lower, tunes_v[:, 0:1], tunes_v[:, 1:2])
    fine = chroma_rows * (lane.astype(jnp.float32) * (2.0 / SLICES))
    first = 2.0 * ((lane & 3).astype(jnp.float32) * LANES + 0.5) / SLICES - 1.0
    coarse = 2.0 * math.pi * tune_rows + chroma_rows * first
    fine_cos, fine_sin = jnp.cos(fine), jnp.sin(fine)
    coarse_cos, coarse_sin = jnp.cos(coarse), jnp.sin(coarse)
    for plane in range(2):
        at = 4 * plane
        base = plane * (2 + 2 * PIECES)
        phases[base] = jnp.broadcast_to(fine_cos[at : at + 1], (8, LANES))
        phases[base + 1] = jnp.broadcast_to(fine_sin[at : at + 1], (8, LANES))
        for piece in range(PIECES):
            spot = (slice(at, at + 1), slice(piece, piece + 1))
            phases[base + 2 + piece] = jnp.broadcast_to(coarse_cos[spot], (8, LANES))
            phases[base + 2 + PIECES + piece] = jnp.broadcast_to(coarse_sin[spot], (8, LANES))

    grid_sum[...] = jnp.zeros_like(grid_sum)
    high_ids = lax.broadcasted_iota(jnp.int32, (HIGH, step_len), 0)
    low_ids = lax.broadcasted_iota(jnp.int32, (LOW, step_len), 0).astype(jnp.bfloat16)
    one, zero = jnp.bfloat16(1), jnp.bfloat16(0)
    shift = LOW.bit_length() - 1

    def deposit(step, _):
        at = pl.multiple_of(step * step_len, step_len)
        where = pl.ds(at, step_len)
        x, y, level = c_buf[0, :, where], c_buf[2, :, where], i_buf[:, where]
        x_low = x - x.astype(jnp.bfloat16).astype(jnp.float32)
        y_low = y - y.astype(jnp.bfloat16).astype(jnp.float32)
        high = lax.shift_right_logical(level, shift)
        low = (level & (LOW - 1)).astype(jnp.float32).astype(jnp.bfloat16)
        for b in range(bunch_dev):
            mask = high_ids == high[b : b + 1]
            values = (1.0, x[b : b + 1], y[b : b + 1], x_low[b : b + 1], y_low[b : b + 1])
            left = jnp.concatenate([jnp.where(mask, v, 0.0) for v in values], axis=0)
            right = jnp.where(low_ids == low[b : b + 1], one, zero)
            grid_sum[b] += lax.dot_general(
                left.astype(jnp.bfloat16),
                right,
                (((1,), (1,)), ((), ())),
                preferred_element_type=jnp.float32,
            )
        return 0

    for plane in (0, 2, 4):
        load(plane, 0).wait()
    lax.fori_loop(0, chunk // step_len, deposit, 0)

    for step in range(1, chunks):
        load(0, step).wait()
        load(2, step).wait()

    def add_up(step, total):
        at = pl.multiple_of(step * chunk, chunk)
        sums = list(total)
        for piece in range(chunk // LANES):
            where = pl.ds(at + piece * LANES, LANES)
            k = piece % 4
            sums[k] = sums[k] + c_buf[0, :, where]
            sums[4 + k] = sums[4 + k] + c_buf[2, :, where]
        return tuple(sums)

    sums = lax.fori_loop(0, chunks, add_up, (zeros,) * 8)
    sum_x = lanes_sum((sums[0] + sums[1]) + (sums[2] + sums[3]))
    sum_y = lanes_sum((sums[4] + sums[5]) + (sums[6] + sums[7]))
    mean = 1.0 / (part_dev * n_dom)
    diagonal = lane == row
    once = jnp.where(me_d == 0, 1.0, 0.0)
    filled = slots[2:3, :]
    tracked = lane[0:1] < bunch_dev
    track_x = rows_sum(jnp.where(diagonal, sum_x, 0.0)) * mean
    track_y = rows_sum(jnp.where(diagonal, sum_y, 0.0)) * mean
    centre_x = filled * jnp.where(tracked, track_x, slots[0:1, :] * once)
    centre_y = filled * jnp.where(tracked, track_y, slots[1:2, :] * once)
    block_own[...] = jnp.where(
        second, lanes_sum(tail_y * centre_y), lanes_sum(tail_x * centre_x)
    )

    pl.semaphore_wait(barrier, n_cycle - 1 + n_dom - 1)

    def block_copy(k):
        return pltpu.make_async_remote_copy(
            src_ref=block_own,
            dst_ref=block_got.at[k],
            send_sem=block_send.at[k],
            recv_sem=block_recv.at[k],
            device_id=cycle_peers[k],
            device_id_type=MESH,
        )

    for k in range(n_cycle - 1):
        block_copy(k).start()

    for step in range(1, chunks):
        load(4, step).wait()
    lax.fori_loop(chunk // step_len, part_dev // step_len, deposit, 0)

    for b in range(bunch_dev):
        part = grid_sum[b]
        kinds = (
            part[0:HIGH],
            part[HIGH : 2 * HIGH] + part[3 * HIGH : 4 * HIGH],
            part[2 * HIGH : 3 * HIGH] + part[4 * HIGH : 5 * HIGH],
        )
        for v in range(3):
            for h in range(HIGH):
                at = v * SLICES + h * LOW
                mine[b : b + 1, at : at + LOW] = kinds[v][h : h + 1]

    def dom_copy(source, target, kind, k):
        return pltpu.make_async_remote_copy(
            src_ref=source,
            dst_ref=target.at[k],
            send_sem=dom_send.at[kind, k],
            recv_sem=dom_recv.at[kind, k],
            device_id=dom_peers[k],
            device_id_type=MESH,
        )

    for k in range(n_dom - 1):
        dom_copy(mine, theirs, 0, k).start()

    carried = block_own[...]
    for k in reversed(range(n_cycle - 1)):
        block_copy(k).wait()
        carried = block_decay * carried + block_got[k]
    pieces = ahead * (carried / closing)
    for j in range(bunch_dev - 1):
        centre = jnp.where(second, centre_y[:, j : j + 1], centre_x[:, j : j + 1])
        gap = jnp.maximum(half - 1 - j, 0).astype(jnp.float32)
        inner = coef_both * jnp.exp(-decay_both * gap) * centre
        pieces = pieces + jnp.where(half > j, inner, 0.0)
    long_row = rows_sum(pieces)
    long_mine[:, 0:LANES] = jnp.broadcast_to(
        lanes_sum(jnp.where(lane == row, long_row, 0.0)), (8, LANES)
    )
    long_mine[:, LANES : 2 * LANES] = jnp.broadcast_to(
        lanes_sum(jnp.where(lane == row + 64, long_row, 0.0)), (8, LANES)
    )

    for k in range(n_dom - 1):
        dom_copy(long_mine, long_theirs, 1, k).start()
    total = mine[...]
    for k in range(n_dom - 1):
        dom_copy(mine, theirs, 0, k).wait()
        total = total + theirs[k]

    small[-1].wait()
    for plane in (1, 3):
        for step in range(chunks):
            load(plane, step).wait()
    scale_moment = SLICES / (part_dev * n_dom)
    for v in range(3):
        padded[v, :, 0:LANES] = zeros
        padded[v, :, LANES:] = total[:, v * SLICES : (v + 1) * SLICES] * scale_moment
    kicks = [jnp.zeros((8, SLICES), jnp.float32)] * 4
    for lag in range(BAND):
        count, mom_x, mom_y = (
            padded[v, :, LANES - lag : LANES - lag + SLICES] for v in range(3)
        )
        for c, source in enumerate((mom_x, count, mom_y, count)):
            kicks[c] = kicks[c] + wake_t[c, lag : lag + 1, :] * source
    long_total = long_mine[...]
    for k in range(n_dom - 1):
        dom_copy(long_mine, long_theirs, 1, k).wait()
        long_total = long_total + long_theirs[k]
    long_x, long_y = long_total[:, 0:1], long_total[:, LANES : LANES + 1]
    tables[0] = kicks[0] + long_x
    tables[1] = kicks[1]
    tables[2] = kicks[2] + long_y
    tables[3] = kicks[3]


def track_kernel(chunk, unroll, c_buf, i_buf, tables, phases, result, o_buf, out_sem):
    part_dev = i_buf.shape[1]
    chunks = part_dev // chunk

    def store(step):
        where = pl.ds(pl.multiple_of(step * chunk, chunk), chunk)
        return pltpu.make_async_copy(
            o_buf.at[:, :, where], result.at[:, :, where], out_sem.at[step]
        )

    def track(step, _):
        where = pl.ds(pl.multiple_of(step * LANES, LANES), LANES)
        level = i_buf[:, where]
        low = level & (LANES - 1)
        piece = lax.shift_right_logical(level, 7)
        odd, upper = (piece & 1) == 1, piece >= 2

        def pick(values):
            return jnp.where(
                upper,
                jnp.where(odd, values[3], values[2]),
                jnp.where(odd, values[1], values[0]),
            )

        def look(table):
            return jnp.take_along_axis(table, low, axis=1)

        def look_up(k):
            return pick(
                [look(tables[k, :, p * LANES : (p + 1) * LANES]) for p in range(PIECES)]
            )

        for plane in range(2):
            base = plane * (2 + 2 * PIECES)
            pos, mom = c_buf[2 * plane, :, where], c_buf[2 * plane + 1, :, where]
            kicked = mom + look_up(2 * plane) + look_up(2 * plane + 1) * pos
            fine_cos, fine_sin = look(phases[base]), look(phases[base + 1])
            coarse_cos = pick([phases[base + 2 + p] for p in range(PIECES)])
            coarse_sin = pick([phases[base + 2 + PIECES + p] for p in range(PIECES)])
            cos = coarse_cos * fine_cos - coarse_sin * fine_sin
            sin = coarse_sin * fine_cos + coarse_cos * fine_sin
            o_buf[2 * plane, :, where] = cos * pos + sin * kicked
            o_buf[2 * plane + 1, :, where] = cos * kicked - sin * pos
        return 0

    each = chunk // LANES
    def run(step, _):
        lax.fori_loop(0, each, lambda k, z: track(step * each + k, z), 0, unroll=unroll)
        store(step).start()
        return 0

    lax.fori_loop(0, chunks, run, 0)
    for step in range(chunks):
        store(step).wait()


def on_device(coords, slice_index, fill, others, wake, decay, coef, tunes, chroma):
    hold = lambda a: pltpu.with_memory_space_constraint(a, pltpu.HBM)
    _, bunch_dev, part_dev = coords.shape
    n_dom, n_cycle = lax.axis_size("dom"), lax.axis_size("bunch")
    chunk, step_len = 8192, 8192
    chunks = part_dev // chunk
    width = 3 * SLICES
    phase_count = 2 * (2 + 2 * PIECES)
    f32 = jnp.float32
    vmem = pl.BlockSpec(memory_space=pltpu.VMEM)
    hbm = pl.BlockSpec(memory_space=pltpu.HBM)
    dma = pltpu.SemaphoreType.DMA
    tables, phases, held, held_index = pl.pallas_call(
        functools.partial(deposit_kernel, n_cycle, n_dom, chunk, step_len),
        out_shape=(
            jax.ShapeDtypeStruct((4, bunch_dev, SLICES), f32),
            jax.ShapeDtypeStruct((phase_count, 8, LANES), f32),
            jax.ShapeDtypeStruct(coords.shape, f32),
            jax.ShapeDtypeStruct((bunch_dev, part_dev), jnp.int32),
        ),
        in_specs=[hbm] * 9,
        out_specs=(vmem,) * 4,
        scratch_shapes=[
            pltpu.VMEM((1, fill.shape[0]), jnp.int32),
            pltpu.VMEM(others.shape, f32),
            pltpu.VMEM((4, BAND, SLICES), f32),
            pltpu.VMEM(decay.shape, f32),
            pltpu.VMEM(coef.shape, f32),
            pltpu.VMEM((1, 2), f32),
            pltpu.VMEM((1, 2), f32),
            pltpu.VMEM((bunch_dev, 5 * HIGH, LOW), f32),
            pltpu.VMEM((8, LANES), f32),
            pltpu.VMEM((8, LANES), f32),
            pltpu.VMEM((8, LANES), f32),
            pltpu.VMEM((n_cycle - 1, 8, LANES), f32),
            pltpu.VMEM((bunch_dev, width), f32),
            pltpu.VMEM((n_dom - 1, bunch_dev, width), f32),
            pltpu.VMEM((bunch_dev, 2 * LANES), f32),
            pltpu.VMEM((n_dom - 1, bunch_dev, 2 * LANES), f32),
            pltpu.VMEM((3, bunch_dev, LANES + SLICES), f32),
            dma((5, chunks)),
            dma((7,)),
            dma((n_cycle - 1,)),
            dma((n_cycle - 1,)),
            dma((2, n_dom - 1)),
            dma((2, n_dom - 1)),
        ],
        compiler_params=pltpu.CompilerParams(
            collective_id=0, has_side_effects=True, vmem_limit_bytes=40 << 20
        ),
        name="deposit",
    )(
        *(
            hold(a)
            for a in (
                coords,
                slice_index,
                fill[None],
                others,
                jnp.swapaxes(wake, 1, 2),
                decay,
                coef,
                tunes[None],
                chroma[None],
            )
        )
    )
    chunk = 4096
    chunks = part_dev // chunk
    return pl.pallas_call(
        functools.partial(track_kernel, chunk, 32),
        out_shape=jax.ShapeDtypeStruct(coords.shape, f32),
        in_specs=[vmem] * 4,
        out_specs=hbm,
        scratch_shapes=[pltpu.VMEM(coords.shape, f32), dma((chunks,))],
        compiler_params=pltpu.CompilerParams(vmem_limit_bytes=40 << 20),
        name="track",
    )(held, held_index, tables, phases)


def solution(mesh):
    placed = (
        P(None, "bunch", "dom"),
        P("bunch", "dom"),
        P("bunch"),
        P(None, "bunch"),
        P(),
        P(),
        P(),
        P(),
        P(),
    )
    return jax.shard_map(
        on_device, mesh=mesh, in_specs=placed, out_specs=P(None, "bunch", "dom"), check_vma=False
    )
```
